32 devices in a mesh: groups: 2 (over x), expert: 16 (over z, y, core).
Axes of the slice: x: 2, y: 2, z: 4, core: 2. Of those that a mesh axis runs over, the one named last changes fastest.
Arguments:
- tokens: bfloat16 [4096, 4096], P(('groups', 'expert')), parts along dimension 0, may hold values from -6 to 6
- cotangent: bfloat16 [4096, 4096], P(('groups', 'expert')), parts along dimension 0, may hold values from -0.29882812 to 0.29882812
- gate_prob: bfloat16 [4096], P(('groups', 'expert')), parts along dimension 0, may hold values from 0.29882812 to 1
- experts_of: int32 [4096, 1], P(('groups', 'expert')), parts along dimension 0, may hold values from 0 to 15; in each aligned block of 128 rows (0 to 127, 128 to 255, ...) at most 10 rows name the same one
- in_weight: bfloat16 [40960, 4096], P('expert'), may hold values from -0.09375 to 0.09375
- out_weight: bfloat16 [40960, 4096], P('expert'), may hold values from -0.125 to 0.125
Outputs:
- gate_grad: float32 [4096], P(('groups', 'expert')), parts along dimension 0
- in_grad: bfloat16 [81920, 4096], P(('groups', 'expert')), parts along dimension 0
- out_grad: bfloat16 [81920, 4096], P(('groups', 'expert')), parts along dimension 0
The draws below stay inside these ranges and needn't reach their ends.
There are 2 independent parts, one for each index of `groups`. The reference program is written for one: setup_inputs(seed, part) draws one part's arguments, and reference() takes and returns one part's arrays. A program takes and returns all parts, laid end to end along the dimension named above; an argument that names none is the same for every part. Nothing has to cross between parts.
Inputs may be any that keep to these rules, and one draw needn't show every extreme that they name: `experts_of`: among the rows of one device no expert is named more than 10 times, and in some device's rows one expert is named exactly 10 times.
All inputs are finite; a program needn't handle non-finite values.
Results may differ from the reference program's by a relative error of at most 0.011.
Values may be sent and summed in bfloat16 or wider, within the bound.
A program may use at most 192 MiB of HBM per device.

```python
import math
import jax
import jax.numpy as jnp
import numpy as np
from jax import lax

D = 4096
FF = 2560
EXPERTS = 16
TOK_DEV = 128
CAP = 10
TOKENS = 2048
N_EXPERT = 16


def block_scale(rng, dims, split, smallest, largest):
    def one(axis_at, blocks):
        steps = jax.random.uniform(jax.random.fold_in(jax.random.fold_in(rng, 6), axis_at), (blocks,), jnp.float32, smallest / len(split), largest / len(split))
        return jnp.repeat(jnp.exp(steps), dims[axis_at] // blocks).reshape((-1,) + (1,) * (len(dims) - axis_at - 1))

    level = one(*split[0])
    for cut in split[1:]:
        level = level * one(*cut)
    return level


def assign_block(rng, own, number, rows, number_of, top, reach, lean):
    order = jax.random.permutation(rng, number_of)
    packed, ordinary = load_shares(number_of, rows * top, reach, lean, True), load_shares(number_of, rows * top, reach, lean, False)
    places = jnp.arange(number_of)

    def named(tallies, rotation):
        used = int((tallies > 0).sum())
        fixed = max(1, used // 4)
        shifted = fixed + (places - fixed + rotation * (used - fixed)) % max(1, number_of - fixed)
        return jnp.zeros((number_of,), jnp.int32).at[order[jnp.where(places < fixed, places, shifted)]].set(jnp.asarray(tallies, jnp.int32))

    tallies = jnp.where(number % 4 == 0, named(packed, number // 4), named(ordinary, number - number // 4 - 1))
    mixed = jax.random.permutation(jax.random.fold_in(own, 3), number_of)
    giver, taker = mixed[0:number_of // 2 * 2:2], mixed[1:number_of // 2 * 2:2]
    room = jnp.minimum(tallies[giver] - 1, reach - tallies[taker]) // 2
    room = jnp.where((giver == order[0]) | (taker == order[0]) | (tallies[taker] == 0), 0, jnp.maximum(room, 0))
    shifted = jax.random.randint(jax.random.fold_in(own, 4), (number_of // 2,), 0, 1 << 20) % (room + 1)
    tallies = tallies.at[giver].add(-shifted).at[taker].add(shifted)
    items = jnp.searchsorted(jnp.cumsum(tallies), jnp.arange(rows * top), side="right").astype(jnp.int32)
    table = items.reshape(top, rows).T
    table = table[jax.random.permutation(jax.random.fold_in(own, 1), rows)]
    rotation = jax.random.randint(jax.random.fold_in(own, 2), (rows, 1), 0, top)
    return jnp.take_along_axis(table, (jnp.arange(top)[None, :] + rotation) % top, axis=1)


def load_shares(number_of, total, limit, skew, full):
    weights = [(1 << 20) // math.isqrt(rank ** skew) + 1 for rank in range(1, number_of + 1)]
    largest = limit if full else min(limit, max(-(-total // number_of), total * weights[0] // sum(weights)))
    least = 1 if total - largest >= number_of - 1 else 0
    holding, spare = [largest] + [least] * (number_of - 1), total - largest - least * (number_of - 1)
    while spare > 0:
        candidates = [i for i in range(1, number_of) if holding[i] < largest] or [i for i in range(1, number_of) if holding[i] < limit]
        mass, left = sum([weights[i] for i in candidates]), spare
        for i in candidates:
            more = min(limit - holding[i], max(1, left * weights[i] // mass), spare)
            holding[i] = holding[i] + more
            spare = spare - more
    return np.array(holding)


def bell_draw(rng, extent, scale, bound, shards=(), kind=jnp.bfloat16):
    entries = jax.random.normal(rng, extent, jnp.float32) * scale
    if len(shards) > 0:
        entries = block_scale(rng, extent, shards, -0.22, 0.18) * entries
    return jnp.clip(entries, min=-bound, max=bound).astype(kind)


def setup_inputs(seed: int = 0, part: int = 0) -> dict:
    arg_keys = jax.random.split(jax.random.key(seed), 7)
    part_splits = jax.random.split(jax.random.fold_in(arg_keys[6], part), 7)
    tokens = bell_draw(part_splits[0], (TOKENS, D), 1.0, 6.0, ((0, 16),))
    cotangent = bell_draw(part_splits[1], (TOKENS, D), 0.05, 0.29882812, ((0, 16),))
    gate_prob = jnp.clip(0.29882812 + 0.7011719 * jax.random.uniform(part_splits[2], (TOKENS,), jnp.float32) ** block_scale(part_splits[2], (TOKENS,), ((0, 16),), -0.2, 0.2), 0.29882812, 1.0).astype(jnp.bfloat16)
    experts_of_keys = jax.random.split(jax.random.fold_in(part_splits[3], 1), TOKENS // TOK_DEV)
    experts_of_turns = jax.random.permutation(jax.random.fold_in(part_splits[3], 3), TOKENS // TOK_DEV)
    experts_of = jax.vmap(lambda own, number: assign_block(jax.random.fold_in(part_splits[3], 2), own, number, TOK_DEV, EXPERTS, 1, CAP, 2))(experts_of_keys, experts_of_turns).reshape((TOKENS, 1))
    in_weight = bell_draw(arg_keys[4], (EXPERTS * FF, D), D ** -0.5, 0.09375, ((0, 16),))
    out_weight = bell_draw(arg_keys[5], (EXPERTS * FF, D), FF ** -0.5, 0.125, ((0, 16),))
    return {"tokens": tokens, "cotangent": cotangent, "gate_prob": gate_prob, "experts_of": experts_of, "in_weight": in_weight, "out_weight": out_weight}


def reference(tokens, cotangent, gate_prob, experts_of, in_weight, out_weight):
    chosen = experts_of[:, 0].astype(jnp.int32)
    most_rows = N_EXPERT * CAP
    count_all = chosen.shape[0]
    labels = jnp.arange(EXPERTS, dtype=jnp.int32)
    onehot = (chosen[:, None] == labels[None, :]).astype(jnp.int32)
    place = jnp.sum((jnp.cumsum(onehot, axis=0) - 1) * onehot, axis=1).astype(jnp.int32)
    flat_place = (chosen * most_rows + place).astype(jnp.int32)
    index = jnp.full((EXPERTS * most_rows,), count_all, jnp.int32)
    index = index.at[flat_place].set(jnp.arange(count_all, dtype=jnp.int32)).reshape(EXPERTS, most_rows)
    padded_tokens = jnp.concatenate([tokens, jnp.zeros((1, D), tokens.dtype)], axis=0)
    padded_grads = jnp.concatenate([cotangent, jnp.zeros((1, D), cotangent.dtype)], axis=0)
    padded_gates = jnp.concatenate([gate_prob, jnp.zeros((1,), gate_prob.dtype)], axis=0)
    stacked_in = in_weight.reshape(EXPERTS, FF, D)
    stacked_out = out_weight.reshape(EXPERTS, FF, D)

    def expert(operands):
        rows, weight_in, weight_out = operands
        rows_tok = padded_tokens[rows]
        rows_grad = padded_grads[rows]
        gate_wide = padded_gates[rows].astype(jnp.float32)[:, None]
        preact = jnp.dot(rows_tok, weight_in.T, preferred_element_type=jnp.float32)
        hidden = jnp.maximum(preact, 0.0).astype(jnp.bfloat16)
        back = jnp.dot(rows_grad, weight_out.T, preferred_element_type=jnp.float32)
        gate_part = jnp.sum(hidden.astype(jnp.float32) * back, axis=1)
        scaled = (gate_wide * rows_grad.astype(jnp.float32)).astype(jnp.bfloat16)
        hidden_grad = jnp.where(preact > 0, gate_wide * back, 0.0).astype(jnp.bfloat16)
        grad_out = jnp.dot(hidden.T, scaled, preferred_element_type=jnp.float32)
        grad_in = jnp.dot(hidden_grad.T, rows_tok, preferred_element_type=jnp.float32)
        return grad_in.astype(jnp.bfloat16), grad_out.astype(jnp.bfloat16), gate_part

    grads_in, grads_out, parts = lax.map(expert, (index, stacked_in, stacked_out))
    gate_grad = jnp.zeros((count_all + 1,), jnp.float32).at[index.reshape(-1)].add(parts.reshape(-1))[:count_all]
    return gate_grad, grads_in.reshape(EXPERTS * FF, D), grads_out.reshape(EXPERTS * FF, D)
```

```python
import functools
import math

import jax
import jax.numpy as jnp
from jax import lax
from jax.experimental import pallas as pl
from jax.experimental.pallas import tpu as pltpu
from jax.sharding import PartitionSpec as P

EXPERTS = 16
SUB = 16
PARTS = 4
MESH = pl.DeviceIdType.MESH
BF = jnp.bfloat16
F32 = jnp.float32


def contract_last(left, right):
    return lax.dot_general(
        left, right, (((1,), (1,)), ((), ())), preferred_element_type=F32
    )


def mm(left, right):
    return jnp.dot(left, right, preferred_element_type=F32)


def iota(shape, dim):
    return lax.broadcasted_iota(jnp.int32, shape, dim)


def hot(cond):
    return jnp.where(cond, 1.0, 0.0).astype(BF)


def exchange(
    n, slabs, cap,
    tok, cot, gate, who, w_in, w_out,
    gate_grad, hid_out, hg_out, tok_out, sc_out,
    stage, send_b, send_a, recv_b, recv_a, win, wout, pre, back,
    stg_tok, stg_sc, ret_s, ret_r,
    in_sem, w_sem, send_sem, recv_sem, out_sem, ret_sem,
):
    me = lax.axis_index("expert")
    count = tok.shape[0]
    chunk = stage.shape[1] // PARTS
    extra = SUB - cap
    rest = cap - extra
    rows = EXPERTS * SUB
    total = n * SUB
    ffn = w_in.shape[0]
    tile = math.gcd(ffn, 512)
    block = 256

    barrier = pltpu.get_barrier_semaphore()

    @pl.loop(1, n)
    def _(i):
        pl.semaphore_signal(
            barrier, inc=1, device_id={"expert": lax.rem(me + i, n)}, device_id_type=MESH
        )

    ins = [
        pltpu.make_async_copy(cot, stage.at[pl.ds(count, count)], in_sem.at[0]),
        pltpu.make_async_copy(tok, stage.at[pl.ds(0, count)], in_sem.at[1]),
    ]
    for c in ins:
        c.start()

    def weights(k):
        cols = pl.ds(k * chunk, chunk)
        return [
            pltpu.make_async_copy(w_in.at[:, cols], win.at[k % 2], w_sem.at[0, k % 2]),
            pltpu.make_async_copy(w_out.at[:, cols], wout.at[k % 2], w_sem.at[1, k % 2]),
        ]

    loads = [weights(k) for k in range(PARTS)]

    chosen = who[...]
    square = (count, count)
    chosen_col = jnp.transpose(jnp.broadcast_to(chosen.astype(F32), square)).astype(jnp.int32)
    earlier = (chosen_col == chosen) & (iota(square, 0) < iota(square, 1))
    place = jnp.sum(jnp.where(earlier, 1.0, 0.0), axis=0, keepdims=True)
    place_col = jnp.transpose(jnp.broadcast_to(place, square)).astype(jnp.int32)
    code = jnp.broadcast_to(chosen * SUB + place.astype(jnp.int32), (rows, count))
    row = iota((rows, count), 0)
    slot = row % SUB
    sel_tok = (code == row) & (slot < cap)
    sel_cot = (code == row - cap) & (slot >= cap)
    sel = jnp.concatenate([hot(sel_tok), hot(sel_cot)], axis=1)
    gates = jnp.sum(
        jnp.where(sel_tok, jnp.broadcast_to(gate[...].astype(F32), (rows, count)), 0.0),
        axis=1, keepdims=True,
    )
    send_b[:, pl.ds(chunk, 128)] = jnp.broadcast_to(gates, (rows, 128)).astype(BF)
    ins[0].wait()
    late = jnp.zeros((rows, chunk), F32)
    for q in range(PARTS):
        pick = hot((slot % PARTS == q) & (code == row - slot + extra + slot // PARTS))
        late = late + mm(pick, stage[pl.ds(count, count), pl.ds(q * chunk, chunk)])
    send_b[:, pl.ds(0, chunk)] = late.astype(BF)
    ins[1].wait()

    pl.semaphore_wait(barrier, n - 1)

    def send(src, dst, at):
        @pl.loop(1, n)
        def _(i):
            to = lax.rem(me + i, n)
            pltpu.make_async_remote_copy(
                src_ref=src.at[pl.ds(pl.multiple_of(to // slabs * SUB, SUB), SUB)],
                dst_ref=dst.at[pl.ds(pl.multiple_of(me * SUB, SUB), SUB)],
                send_sem=send_sem.at[at],
                recv_sem=recv_sem.at[at],
                device_id={"expert": to},
                device_id_type=MESH,
            ).start()

        dst[pl.ds(pl.multiple_of(me * SUB, SUB), SUB), :] = src[
            pl.ds(pl.multiple_of(me // slabs * SUB, SUB), SUB), :
        ]

    def arrived(dst, at):
        part = dst.at[pl.ds(0, total - SUB)]
        pltpu.make_async_copy(part, part, recv_sem.at[at]).wait()

    def left(dst, at):
        part = dst.at[pl.ds(0, total - SUB)]
        pltpu.make_async_copy(part, part, send_sem.at[at]).wait()

    send(send_b, recv_b, PARTS)
    for k in range(PARTS):
        send_a[k] = mm(sel, stage[:, pl.ds(k * chunk, chunk)]).astype(BF)
        send(send_a.at[k], recv_a.at[k], k)
    for k in range(2):
        for c in loads[k]:
            c.start()

    arrived(recv_b, PARTS)
    lane0 = hot(iota((8, 128), 1) == 0)
    gate_row = contract_last(lane0, recv_b[:, pl.ds(chunk, 128)])[0:1]

    def outs(k):
        cols = pl.ds(k * chunk, chunk)
        return [
            pltpu.make_async_copy(stg_tok.at[k % 2], tok_out.at[:, cols], out_sem.at[0, k % 2]),
            pltpu.make_async_copy(stg_sc.at[k % 2], sc_out.at[:, cols], out_sem.at[1, k % 2]),
        ]

    writes = [outs(k) for k in range(PARTS)]
    r0 = iota((block, block), 0)
    r1 = iota((block, block), 1)
    j = r0 % SUB
    keep = hot((r0 == r1) & (j < cap))
    first = hot((r1 == r0 + cap) & (j < extra))
    part_sum = jnp.zeros((8, total), F32)
    for k in range(PARTS):
        for c in loads[k]:
            c.wait()
        if k >= 2:
            for c in writes[k - 2]:
                c.wait()
        arrived(recv_a.at[k], k)
        second = hot((j >= extra) & (j < cap) & (r1 == r0 - j + (j - extra) * PARTS + k))

        @pl.loop(0, total // block)
        def _(b):
            at = pl.ds(pl.multiple_of(b * block, block), block)
            mixed = recv_a[k, at, :]
            gate_col = recv_b[at, pl.ds(chunk, 128)].astype(F32)[:, 0:1]
            stg_tok[k % 2, at, :] = mm(keep, mixed).astype(BF)
            grads = mm(first, mixed) + mm(second, recv_b[at, pl.ds(0, chunk)])
            recv_a[k, at, :] = grads.astype(BF)
            stg_sc[k % 2, at, :] = (gate_col * grads).astype(BF)

        for c in writes[k]:
            c.start()

        def step(i, acc):
            at = pl.ds(pl.multiple_of(i * tile, tile), tile)
            p = contract_last(win[k % 2, at, :], stg_tok[k % 2])
            g = contract_last(wout[k % 2, at, :], recv_a[k])
            if k > 0:
                p = p + pre[at, :]
                g = g + back[at, :]
            if k < PARTS - 1:
                pre[at, :] = p
                back[at, :] = g
                return acc
            hidden = jnp.maximum(p, 0.0).astype(BF)
            hid_out[at, :] = hidden
            hg_out[at, :] = jnp.where(p > 0, gate_row * g, 0.0).astype(BF)
            share = hidden.astype(F32) * g
            return acc + jnp.sum(share.reshape(tile // 8, 8, total), axis=0)

        part_sum = lax.fori_loop(0, ffn // tile, step, part_sum)
        if k + 2 < PARTS:
            for c in loads[k + 2]:
                c.start()

    shares = jnp.sum(part_sum, axis=0, keepdims=True)
    per_tile = 128 // SUB
    for h in range(total // 128):
        ret_s[h] = jnp.broadcast_to(shares[:, h * 128:(h + 1) * 128], (8, 128))

    @pl.loop(1, n)
    def _(i):
        to = lax.rem(me + i, n)
        pltpu.make_async_remote_copy(
            src_ref=ret_s.at[to // per_tile],
            dst_ref=ret_r.at[me],
            send_sem=ret_sem.at[0],
            recv_sem=ret_sem.at[1],
            device_id={"expert": to},
            device_id_type=MESH,
        ).start()

    ret_r[me] = ret_s[me // per_tile]
    for k in range(PARTS - 2, PARTS):
        for c in writes[k]:
            c.wait()
    for k in range(PARTS):
        left(recv_a.at[k], k)
    left(recv_b, PARTS)
    tail = ret_r.at[pl.ds(0, n - 1)]
    for s in range(2):
        pltpu.make_async_copy(tail, tail, ret_sem.at[s]).wait()

    found = jnp.zeros((count, 128), F32)
    for d in range(n):
        found = found + jnp.where(chosen_col == d // slabs, ret_r[d][0:1], 0.0)
    mine = iota((count, 128), 1) == place_col + SUB * lax.rem(me, per_tile)
    column = jnp.sum(jnp.where(mine, found, 0.0), axis=1, keepdims=True)
    gate_grad[...] = jnp.transpose(jnp.broadcast_to(column, square))[0:1]


def outer(hid, hg, tok, scaled, in_grad, out_grad):
    out_grad[...] = mm(hid[...], scaled[...]).astype(BF)
    in_grad[...] = mm(hg[...], tok[...]).astype(BF)


def per_device(tokens, cotangent, gate_prob, experts_of, in_weight, out_weight):
    n = lax.axis_size("expert")
    slabs = n // EXPERTS
    count, width = tokens.shape
    ffn = in_weight.shape[0]
    cap = 5 * count // (4 * EXPERTS)
    chunk = width // PARTS
    rows = EXPERTS * SUB
    total = n * SUB
    anywhere = pl.BlockSpec(memory_space=pl.ANY)
    vmem = pl.BlockSpec(memory_space=pltpu.VMEM)
    dma = pltpu.SemaphoreType.DMA
    gate_grad, hid, hg, tok, scaled = pl.pallas_call(
        functools.partial(exchange, n, slabs, cap),
        out_shape=(
            jax.ShapeDtypeStruct((1, count), F32),
            jax.ShapeDtypeStruct((ffn, total), BF),
            jax.ShapeDtypeStruct((ffn, total), BF),
            jax.ShapeDtypeStruct((total, width), BF),
            jax.ShapeDtypeStruct((total, width), BF),
        ),
        in_specs=[anywhere, anywhere, vmem, vmem, anywhere, anywhere],
        out_specs=(vmem, vmem, vmem, anywhere, anywhere),
        scratch_shapes=[
            pltpu.VMEM((2 * count, width), BF),
            pltpu.VMEM((rows, chunk + 128), BF),
            pltpu.VMEM((PARTS, rows, chunk), BF),
            pltpu.VMEM((total, chunk + 128), BF),
            pltpu.VMEM((PARTS, total, chunk), BF),
            pltpu.VMEM((2, ffn, chunk), BF),
            pltpu.VMEM((2, ffn, chunk), BF),
            pltpu.VMEM((ffn, total), F32),
            pltpu.VMEM((ffn, total), F32),
            pltpu.VMEM((2, total, chunk), BF),
            pltpu.VMEM((2, total, chunk), BF),
            pltpu.VMEM((total // 128, 8, 128), F32),
            pltpu.VMEM((n, 8, 128), F32),
            dma((2,)),
            dma((2, 2)),
            dma((PARTS + 1,)),
            dma((PARTS + 1,)),
            dma((2, 2)),
            dma((2,)),
        ],
        compiler_params=pltpu.CompilerParams(
            collective_id=0, has_side_effects=True, vmem_limit_bytes=62 * 2**20
        ),
        name="exchange",
    )(
        tokens, cotangent, gate_prob.reshape(1, count), experts_of.reshape(1, count),
        in_weight, out_weight,
    )
    tile = math.gcd(ffn, 256)
    cols = min(width, width * 256 // total)
    left = pl.BlockSpec((tile, total), lambda c, i: (i, 0))
    right = pl.BlockSpec((total, cols), lambda c, i: (0, c))
    result = pl.BlockSpec((tile, cols), lambda c, i: (i, c))
    grad = jax.ShapeDtypeStruct((ffn, width), BF)
    in_grad, out_grad = pl.pallas_call(
        outer,
        grid=(width // cols, ffn // tile),
        out_shape=(grad, grad),
        in_specs=[left, left, right, right],
        out_specs=(result, result),
        compiler_params=pltpu.CompilerParams(vmem_limit_bytes=56 * 2**20),
        name="outer",
    )(hid, hg, tok, scaled)
    return (gate_grad.reshape(count), in_grad, out_grad)


def solution(mesh):
    return jax.shard_map(
        per_device,
        mesh=mesh,
        in_specs=(
            P(("groups", "expert"), None),
            P(("groups", "expert"), None),
            P(("groups", "expert")),
            P(("groups", "expert"), None),
            P("expert", None),
            P("expert", None),
        ),
        out_specs=(
            P(("groups", "expert")),
            P(("groups", "expert"), None),
            P(("groups", "expert"), None),
        ),
        check_vma=False,
    )
```

```python
import functools
import math

import jax
import jax.numpy as jnp
from jax import lax
from jax.experimental import pallas as pl
from jax.experimental.pallas import tpu as pltpu
from jax.sharding import PartitionSpec as P

EXPERTS = 16
SUB = 16
PARTS = 4
MESH = pl.DeviceIdType.MESH
BF = jnp.bfloat16
F32 = jnp.float32


def contract_last(left, right):
    return lax.dot_general(
        left, right, (((1,), (1,)), ((), ())), preferred_element_type=F32
    )


def mm(left, right):
    return jnp.dot(left, right, preferred_element_type=F32)


def iota(shape, dim):
    return lax.broadcasted_iota(jnp.int32, shape, dim)


def hot(cond):
    return jnp.where(cond, 1.0, 0.0).astype(BF)


def exchange(
    n, slabs, cap,
    tok, cot, gate, who, w_in, w_out,
    gate_grad, hid_out, hg_out, tok_out, sc_out,
    stage, send_b, send_a, recv_b, recv_a, win, wout, pre, back,
    stg_tok, stg_sc, hid, hg, gate_s, gate_r, gate_cols, ret_s, ret_r,
    in_sem, w_sem, send_sem, recv_sem, out_sem, tile_sem, gate_sem, ret_sem,
):
    me = lax.axis_index("expert")
    count = tok.shape[0]
    chunk = stage.shape[1] // PARTS
    extra = SUB - cap
    rest = cap - extra
    rows = EXPERTS * SUB
    total = n * SUB
    ffn = w_in.shape[0]
    tile = math.gcd(ffn, 512)
    block = 256
    cut = chunk * 3 // 4
    steps = [(k, 0, chunk) for k in range(PARTS - 1)]
    steps += [(PARTS - 1, 0, cut), (PARTS - 1, cut, chunk - cut)]
    last = len(steps) - 1

    barrier = pltpu.get_barrier_semaphore()

    @pl.loop(1, n)
    def _(i):
        pl.semaphore_signal(
            barrier, inc=1, device_id={"expert": lax.rem(me + i, n)}, device_id_type=MESH
        )

    ins = [
        pltpu.make_async_copy(cot, stage.at[pl.ds(count, count)], in_sem.at[0]),
        pltpu.make_async_copy(tok, stage.at[pl.ds(0, count)], in_sem.at[1]),
    ]
    for c in ins:
        c.start()

    def weights(k):
        cols = pl.ds(k * chunk, chunk)
        return [
            pltpu.make_async_copy(w_in.at[:, cols], win.at[k % 2], w_sem.at[0, k % 2]),
            pltpu.make_async_copy(w_out.at[:, cols], wout.at[k % 2], w_sem.at[1, k % 2]),
        ]

    loads = [weights(k) for k in range(PARTS)]

    chosen = who[...]
    square = (count, count)
    chosen_col = jnp.transpose(jnp.broadcast_to(chosen.astype(F32), square)).astype(jnp.int32)
    earlier = (chosen_col == chosen) & (iota(square, 0) < iota(square, 1))
    place = jnp.sum(jnp.where(earlier, 1.0, 0.0), axis=0, keepdims=True)
    place_col = jnp.transpose(jnp.broadcast_to(place, square)).astype(jnp.int32)
    code = jnp.broadcast_to(chosen * SUB + place.astype(jnp.int32), (rows, count))
    row = iota((rows, count), 0)
    slot = row % SUB
    sel_tok = (code == row) & (slot < cap)
    sel_cot = (code == row - cap) & (slot >= cap)
    sel = jnp.concatenate([hot(sel_tok), hot(sel_cot)], axis=1)
    ins[0].wait()
    late = jnp.zeros((rows, chunk), F32)
    for q in range(PARTS):
        pick = hot((slot % PARTS == q) & (code == row - slot + extra + slot // PARTS))
        late = late + mm(pick, stage[pl.ds(count, count), pl.ds(q * chunk, chunk)])
    send_b[...] = late.astype(BF)
    ins[1].wait()

    pl.semaphore_wait(barrier, n - 1)

    def mine(ref, cols):
        return ref.at[pl.ds(pl.multiple_of(me * SUB, SUB), SUB), cols]

    def send(src, dst, cols, at):
        @pl.loop(1, n)
        def _(i):
            to = lax.rem(me + i, n)
            pltpu.make_async_remote_copy(
                src_ref=src.at[pl.ds(pl.multiple_of(to // slabs * SUB, SUB), SUB), cols],
                dst_ref=mine(dst, cols),
                send_sem=send_sem.at[at],
                recv_sem=recv_sem.at[at],
                device_id={"expert": to},
                device_id_type=MESH,
            ).start()

        dst[pl.ds(pl.multiple_of(me * SUB, SUB), SUB), cols] = src[
            pl.ds(pl.multiple_of(me // slabs * SUB, SUB), SUB), cols
        ]

    def finish(ref, sem):
        pltpu.make_async_copy(ref, ref, sem).wait()

    def others(dst, cols):
        return dst.at[pl.ds(0, total - SUB), cols]

    def send_rows(src, dst, pick, sem):
        @pl.loop(1, n)
        def _(i):
            to = lax.rem(me + i, n)
            pltpu.make_async_remote_copy(
                src_ref=src.at[pick(to)],
                dst_ref=dst.at[me],
                send_sem=sem.at[0],
                recv_sem=sem.at[1],
                device_id={"expert": to},
                device_id_type=MESH,
            ).start()

        dst[me] = src[pick(me)]

    whole = pl.ds(0, chunk)
    send(send_b, recv_b, whole, last + 1)
    for s, (k, start, size) in enumerate(steps):
        if start == 0:
            send_a[k] = mm(sel, stage[:, pl.ds(k * chunk, chunk)]).astype(BF)
        send(send_a.at[k], recv_a.at[k], pl.ds(start, size), s)
        if s == 0:
            gate_col = jnp.transpose(jnp.broadcast_to(gate[...].astype(F32), square))
            lane = iota((count, 128), 1) % SUB
            at_slot = (place_col == lane) & (lane < cap)
            for e in range(EXPERTS):
                picked = jnp.where(at_slot & (chosen_col == e), gate_col, 0.0)
                gate_s[e] = jnp.sum(picked, axis=0, keepdims=True)
            send_rows(gate_s, gate_r, lambda to: to // slabs, gate_sem)
            for i in range(2):
                for c in loads[i]:
                    c.start()

    per_tile = 128 // SUB
    finish(gate_r.at[pl.ds(0, n - 1)], gate_sem.at[1])
    lane = iota((1, 128), 1) // SUB
    gate_rows = []
    for h in range(total // 128):
        piece = jnp.zeros((1, 128), F32)
        for i in range(per_tile):
            piece = piece + jnp.where(lane == i, gate_r[h * per_tile + i], 0.0)
        gate_rows.append(piece)
        gate_cols[pl.ds(h * 128, 128), :] = jnp.transpose(jnp.broadcast_to(piece, (128, 128)))
    gate_row = jnp.concatenate(gate_rows, axis=1)
    finish(others(recv_b, whole), recv_sem.at[last + 1])

    def outs(k):
        cols = pl.ds(k * chunk, chunk)
        return [
            pltpu.make_async_copy(stg_tok.at[k % 2], tok_out.at[:, cols], out_sem.at[0, k % 2]),
            pltpu.make_async_copy(stg_sc.at[k % 2], sc_out.at[:, cols], out_sem.at[1, k % 2]),
        ]

    writes = [outs(k) for k in range(PARTS)]
    r0 = iota((block, block), 0)
    r1 = iota((block, block), 1)
    j = r0 % SUB
    keep = hot((r0 == r1) & (j < cap))
    first = hot((r1 == r0 + cap) & (j < extra))
    part_sum = jnp.zeros((8, total), F32)

    def tiles(i):
        at = pl.ds(pl.multiple_of(i * tile, tile), tile)
        return [
            pltpu.make_async_copy(hid.at[at], hid_out.at[at], tile_sem.at[0, i]),
            pltpu.make_async_copy(hg.at[at], hg_out.at[at], tile_sem.at[1, i]),
        ]

    for s, (k, start, size) in enumerate(steps):
        cols = pl.ds(start, size)
        if start == 0:
            for c in loads[k]:
                c.wait()
            if k >= 2:
                for c in writes[k - 2]:
                    c.wait()
        finish(others(recv_a.at[k], cols), recv_sem.at[s])
        second = hot((j >= extra) & (j < cap) & (r1 == r0 - j + (j - extra) * PARTS + k))

        @pl.loop(0, total // block)
        def _(b):
            at = pl.ds(pl.multiple_of(b * block, block), block)
            mixed = recv_a[k, at, cols]
            stg_tok[k % 2, at, cols] = mm(keep, mixed).astype(BF)
            grads = mm(first, mixed) + mm(second, recv_b[at, cols])
            recv_a[k, at, cols] = grads.astype(BF)
            stg_sc[k % 2, at, cols] = (gate_cols[at, :][:, 0:1] * grads).astype(BF)

        if start + size == chunk:
            for c in writes[k]:
                c.start()

        def step(i, acc):
            at = pl.ds(pl.multiple_of(i * tile, tile), tile)
            p = contract_last(win[k % 2, at, cols], stg_tok[k % 2, :, cols])
            g = contract_last(wout[k % 2, at, cols], recv_a[k, :, cols])
            if s > 0:
                p = p + pre[at, :]
                g = g + back[at, :]
            if s < last:
                pre[at, :] = p
                back[at, :] = g
                return acc
            hidden = jnp.maximum(p, 0.0).astype(BF)
            hid[at, :] = hidden
            hg[at, :] = jnp.where(p > 0, gate_row * g, 0.0).astype(BF)
            for c in tiles(i):
                c.start()
            share = hidden.astype(F32) * g
            return acc + jnp.sum(share.reshape(tile // 8, 8, total), axis=0)

        part_sum = lax.fori_loop(0, ffn // tile, step, part_sum)
        if start + size == chunk and k + 2 < PARTS:
            for c in loads[k + 2]:
                c.start()

    shares = jnp.sum(part_sum, axis=0, keepdims=True)
    for h in range(total // 128):
        ret_s[h] = shares[:, h * 128:(h + 1) * 128]

    send_rows(ret_s, ret_r, lambda to: to // per_tile, ret_sem)
    for k in range(PARTS - 2, PARTS):
        for c in writes[k]:
            c.wait()

    @pl.loop(0, ffn // tile)
    def _(i):
        for c in tiles(i):
            c.wait()

    for s, (k, start, size) in enumerate(steps):
        finish(others(recv_a.at[k], pl.ds(start, size)), send_sem.at[s])
    finish(others(recv_b, whole), send_sem.at[last + 1])
    finish(gate_r.at[pl.ds(0, n - 1)], gate_sem.at[0])
    for i in range(2):
        finish(ret_r.at[pl.ds(0, n - 1)], ret_sem.at[i])

    found = jnp.zeros((count, 128), F32)
    for d in range(n):
        found = found + jnp.where(chosen_col == d // slabs, ret_r[d], 0.0)
    own = iota((count, 128), 1) == place_col + SUB * lax.rem(me, per_tile)
    column = jnp.sum(jnp.where(own, found, 0.0), axis=1, keepdims=True)
    gate_grad[...] = jnp.transpose(jnp.broadcast_to(column, square))[0:1]


def outer(hid, hg, tok, scaled, gate_in, in_grad, out_grad, gate_out):
    gate_out[...] = gate_in[...]
    out_grad[...] = mm(hid[...], scaled[...]).astype(BF)
    in_grad[...] = mm(hg[...], tok[...]).astype(BF)


def per_device(tokens, cotangent, gate_prob, experts_of, in_weight, out_weight):
    n = lax.axis_size("expert")
    slabs = n // EXPERTS
    count, width = tokens.shape
    ffn = in_weight.shape[0]
    cap = 5 * count // (4 * EXPERTS)
    chunk = width // PARTS
    rows = EXPERTS * SUB
    total = n * SUB
    anywhere = pl.BlockSpec(memory_space=pl.ANY)
    vmem = pl.BlockSpec(memory_space=pltpu.VMEM)
    dma = pltpu.SemaphoreType.DMA
    gate_grad, hid, hg, tok, scaled = pl.pallas_call(
        functools.partial(exchange, n, slabs, cap),
        out_shape=(
            jax.ShapeDtypeStruct((1, count), F32),
            jax.ShapeDtypeStruct((ffn, total), BF),
            jax.ShapeDtypeStruct((ffn, total), BF),
            jax.ShapeDtypeStruct((total, width), BF),
            jax.ShapeDtypeStruct((total, width), BF),
        ),
        in_specs=[anywhere, anywhere, vmem, vmem, anywhere, anywhere],
        out_specs=(vmem,) + (anywhere,) * 4,
        scratch_shapes=[
            pltpu.VMEM((2 * count, width), BF),
            pltpu.VMEM((rows, chunk), BF),
            pltpu.VMEM((PARTS, rows, chunk), BF),
            pltpu.VMEM((total, chunk), BF),
            pltpu.VMEM((PARTS, total, chunk), BF),
            pltpu.VMEM((2, ffn, chunk), BF),
            pltpu.VMEM((2, ffn, chunk), BF),
            pltpu.VMEM((ffn, total), F32),
            pltpu.VMEM((ffn, total), F32),
            pltpu.VMEM((2, total, chunk), BF),
            pltpu.VMEM((2, total, chunk), BF),
            pltpu.VMEM((ffn, total), BF),
            pltpu.VMEM((ffn, total), BF),
            pltpu.VMEM((EXPERTS, 1, 128), F32),
            pltpu.VMEM((n, 1, 128), F32),
            pltpu.VMEM((total, 128), F32),
            pltpu.VMEM((total // 128, 1, 128), F32),
            pltpu.VMEM((n, 1, 128), F32),
            dma((2,)),
            dma((2, 2)),
            dma((PARTS + 2,)),
            dma((PARTS + 2,)),
            dma((2, 2)),
            dma((2, ffn // math.gcd(ffn, 512))),
            dma((2,)),
            dma((2,)),
        ],
        compiler_params=pltpu.CompilerParams(
            collective_id=0, has_side_effects=True, vmem_limit_bytes=(42 if total <= 256 else 62) * 2**20
        ),
        name="exchange",
    )(
        tokens, cotangent, gate_prob.reshape(1, count), experts_of.reshape(1, count),
        in_weight, out_weight,
    )
    tile = math.gcd(ffn, 256)
    cols = min(width, width * 256 // total)
    left = pl.BlockSpec((tile, total), lambda c, i: (i, 0))
    right = pl.BlockSpec((total, cols), lambda c, i: (0, c))
    result = pl.BlockSpec((tile, cols), lambda c, i: (i, c))
    small = pl.BlockSpec((1, count), lambda c, i: (0, 0))
    grad = jax.ShapeDtypeStruct((ffn, width), BF)
    in_grad, out_grad, gate_grad = pl.pallas_call(
        outer,
        grid=(width // cols, ffn // tile),
        out_shape=(grad, grad, jax.ShapeDtypeStruct((1, count), F32)),
        in_specs=[left, left, right, right, small],
        out_specs=(result, result, small),
        compiler_params=pltpu.CompilerParams(vmem_limit_bytes=(28 if total <= 256 else 56) * 2**20),
        name="outer",
    )(hid, hg, tok, scaled, gate_grad)
    return (gate_grad.reshape(count), in_grad, out_grad)


def solution(mesh):
    return jax.shard_map(
        per_device,
        mesh=mesh,
        in_specs=(
            P(("groups", "expert"), None),
            P(("groups", "expert"), None),
            P(("groups", "expert")),
            P(("groups", "expert"), None),
            P("expert", None),
            P("expert", None),
        ),
        out_specs=(
            P(("groups", "expert")),
            P(("groups", "expert"), None),
            P(("groups", "expert"), None),
        ),
        check_vma=False,
    )
```
